1024 devices in a mesh: dp: 64 (over y_hi, x, core), expert: 16 (over z, y_lo).
Axes of the slice: x: 8, y: 8 (y_hi: 4, y_lo: 2; y = y_hi * 2 + y_lo), z: 8, core: 2. Of those that a mesh axis runs over, the one named last changes fastest.
Arguments:
- token_values: bfloat16 [131072, 3584], P(('dp', 'expert')), may hold values from -24 to 24
- block_scales: bfloat16 [131072, 28], P(('dp', 'expert')), may hold values from 0.25 to 4
- route_ids: int32 [131072, 8], P(('dp', 'expert')), may hold values from 0 to 255, as said below
- route_slots: int32 [131072], P(('dp', 'expert')), may hold values from 0 to 127, as said below
- router_logits: float32 [131072, 256], P(('dp', 'expert')), may hold values from -8 to 8
- expert_outputs: bfloat16 [98304, 3584], P(('dp', 'expert')), may hold values from -6 to 6
- output_grad: bfloat16 [131072, 3584], P(('dp', 'expert')), may hold values from -0.09375 to 0.09375
Outputs:
- expert_inputs: bfloat16 [98304, 3584], P(('dp', 'expert'))
- slot_expert: int32 [98304], P(('dp', 'expert'))
- gate_grads: float32 [131072], P(('dp', 'expert'))
- router_grad: float32 [3584, 256], P('dp', 'expert')
The draws below stay inside these ranges and needn't reach their ends.
Inputs may be any that keep to these rules, and one draw needn't show every extreme that they name: `route_ids`: each row names 8 different experts; expert e is owned by index e // 16 of the expert axis. Only the first expert of a row is dispatched here; on every device some owner is named first by 6 or more of its tokens. `route_slots`: among one device's 128 tokens whose first expert lies on one owner, in token order, the slots are 0, 1, 2 and so on; pairs with slot 6 or more are dropped.
All inputs are finite; a program needn't handle non-finite values.
Results may differ from the reference program's by a relative error of at most 0.0049.
Values may be sent and summed in bfloat16 or wider, within the bound.
No kernel may reach another device: no remote copies, remote signals or barrier semaphores. Data moves between devices by JAX's collectives and lax.ppermute only.
A program may use at most 128 MiB of HBM per device.

```python
import math
import jax
import jax.numpy as jnp
from jax import lax

D = 3584
TOPK = 8
EXP_DEV = 16
TOK_DEV = 128
EXPERTS = 256
TOKENS = 131072
BLOCKS = 28
CAP = 6
SLOTS_ALL = 98304
N_EXPERT = 16


def route_pair(key):
    blocks = TOKENS // TOK_DEV
    owner_ids = jax.random.randint(jax.random.fold_in(key, 11), (blocks, TOK_DEV), 0, N_EXPERT)
    forced = jax.random.randint(jax.random.fold_in(key, 12), (blocks,), 0, N_EXPERT)
    rank_noise = jax.random.randint(jax.random.fold_in(key, 13), (blocks, TOK_DEV), 0, 1 << 20)
    rank_score = rank_noise * TOK_DEV + jnp.arange(TOK_DEV, dtype=jnp.int32)[None, :]
    ordering = jnp.argsort(rank_score, axis=1)
    ranks = jnp.argsort(ordering, axis=1)
    first_block = (jnp.arange(blocks, dtype=jnp.int32) == 0)[:, None]
    owner_ids = jnp.where((ranks < CAP) | first_block, forced[:, None], owner_ids).astype(jnp.int32)
    local_ids = jax.random.randint(jax.random.fold_in(key, 14), (TOKENS,), 0, EXP_DEV)
    lead_ids = (owner_ids.reshape(-1) * EXP_DEV + local_ids).astype(jnp.int32)
    noise = jax.random.randint(jax.random.fold_in(key, 15), (TOKENS, EXPERTS), 0, 1 << 20)
    columns = jnp.arange(EXPERTS, dtype=jnp.int32)[None, :]
    score = noise * EXPERTS + columns
    score = jnp.where(columns == lead_ids[:, None], -1, score)
    chosen = jnp.argsort(score, axis=1)[:, :TOPK].astype(jnp.int32)
    onehot = (owner_ids[:, :, None] == jnp.arange(N_EXPERT, dtype=jnp.int32)[None, None, :]).astype(jnp.int32)
    before = jnp.cumsum(onehot, axis=1) - onehot
    slots = jnp.sum(before * onehot, axis=2).reshape(TOKENS).astype(jnp.int32)
    return (chosen, slots)


def draw_route_ids(key, part):
    paired = route_pair(key)
    return paired[0]


def draw_route_slots(key, part):
    paired = route_pair(key)
    return paired[1]


def spiked(entries, own_key, source, target, parts, factor):
    def block_of(position):
        return (jnp.arange(entries.shape[position]) // (entries.shape[position] // parts)).reshape((-1,) + (1,) * (entries.ndim - 1 - position))

    one_side = jax.random.permutation(own_key, parts)[block_of(target)]
    far = (block_of(target) + parts // 2) % parts
    return jnp.where((block_of(source) == one_side) | (block_of(source) == far), factor * entries, entries)


def steps_of(key, extent, shards, least, top_value):
    loudness = 1.0
    for dim, parts in shards:
        steps = jax.random.uniform(jax.random.fold_in(jax.random.fold_in(key, 6), dim), (parts,), jnp.float32, least / len(shards), top_value / len(shards))
        loudness = loudness * jnp.repeat(jnp.exp(steps), extent[dim] // parts).reshape((-1,) + (1,) * (len(extent) - 1 - dim))
    return loudness


def centred(rng, dims, width, most, shards=(), kind=jnp.bfloat16):
    loudness = steps_of(rng, dims, shards, -0.22, 0.18) if shards else 1.0
    drawn = jax.random.normal(rng, dims, jnp.float32) * width * loudness
    return jnp.minimum(jnp.maximum(drawn, -most), most).astype(kind)


def heavy_noise(key, shape, scale, most, shards, heavy, held_as=jnp.bfloat16):
    result = scale * jax.random.normal(key, shape, jnp.float32)
    if shards:
        result = result * steps_of(key, shape, shards, -0.22, 0.18)
    return jnp.clip(spiked(result, jax.random.fold_in(key, 3), *heavy), -most, most).astype(held_as)


def setup_inputs(seed: int = 0) -> dict:
    streams_of = jax.random.split(jax.random.key(seed), 8)
    token_values = heavy_noise(streams_of[0], (TOKENS, D), 1.0, 24.0, ((0, 1024),), (0, 1, 512, 6.0))
    block_scales = jnp.clip(jnp.exp(math.log(4.0) - 2.7725887 * jax.random.uniform(streams_of[1], (TOKENS, BLOCKS), jnp.float32) ** steps_of(streams_of[1], (TOKENS, BLOCKS), ((0, 1024),), -0.2, 0.2)), 0.25, 4.0).astype(jnp.bfloat16)
    route_ids = draw_route_ids(jax.random.fold_in(streams_of[7], 71), 0)
    route_slots = draw_route_slots(jax.random.fold_in(streams_of[7], 71), 0)
    router_logits = centred(streams_of[4], (TOKENS, EXPERTS), 2.0, 8.0, ((0, 1024),), jnp.float32)
    expert_outputs = centred(streams_of[5], (SLOTS_ALL, D), 1.0, 6.0, ((0, 1024),))
    output_grad = centred(streams_of[6], (TOKENS, D), D ** -0.5, 0.09375, ((0, 1024),))
    return dict(token_values=token_values, block_scales=block_scales, route_ids=route_ids, route_slots=route_slots, router_logits=router_logits, expert_outputs=expert_outputs, output_grad=output_grad)


routed_scale = 2.5


def reference(token_values, block_scales, route_ids, route_slots, router_logits, expert_outputs, output_grad):
    row_total = token_values.shape[0]
    positions = jnp.arange(row_total, dtype=jnp.int32)
    source_block = positions // TOK_DEV
    group_id = source_block // N_EXPERT
    source = source_block % N_EXPERT
    lead_ids = route_ids[:, 0]
    inside = route_slots < CAP
    owner_id = group_id * N_EXPERT + lead_ids // EXP_DEV
    slot_rows = jnp.where(inside, owner_id * (N_EXPERT * CAP) + source * CAP + route_slots, SLOTS_ALL).astype(jnp.int32)
    widened = jnp.repeat(block_scales.astype(jnp.float32), 128, axis=1)
    dequant = (token_values.astype(jnp.float32) * widened).astype(jnp.bfloat16)
    expert_inputs = jnp.zeros((SLOTS_ALL, D), jnp.bfloat16).at[slot_rows].set(dequant, mode="drop")
    slot_expert = jnp.full((SLOTS_ALL,), -1, jnp.int32).at[slot_rows].set((lead_ids % EXP_DEV).astype(jnp.int32), mode="drop")
    clipped = jnp.minimum(slot_rows, SLOTS_ALL - 1).astype(jnp.int32)
    fetched = jnp.where(inside[:, None], expert_outputs[clipped], jnp.zeros((), jnp.bfloat16))
    gate_grads = jnp.sum(output_grad.astype(jnp.float32) * fetched.astype(jnp.float32), axis=1)
    chosen = jnp.take_along_axis(router_logits, route_ids, axis=1)
    affinity = jax.nn.sigmoid(chosen)
    affinity_sum = jnp.sum(affinity, axis=1, keepdims=True)
    lead_mask = (jnp.arange(TOPK, dtype=jnp.int32) == 0).astype(jnp.float32)[None, :]
    lead_share = affinity[:, 0:1] / affinity_sum
    aff_grad = routed_scale * gate_grads[:, None] * (lead_mask - lead_share) / affinity_sum
    logit_term = aff_grad * affinity * (1.0 - affinity)
    logit_grad = jnp.zeros((row_total, EXPERTS), jnp.float32).at[positions[:, None], route_ids].add(logit_term).astype(jnp.bfloat16)
    router_grad = lax.dot_general(dequant, logit_grad, (((0,), (0,)), ((), ())), preferred_element_type=jnp.float32)
    return expert_inputs, slot_expert, gate_grads, router_grad
```

```python
import jax
import jax.numpy as jnp
import numpy as np
from jax import lax
from jax.experimental import pallas as pl
from jax.experimental.pallas import tpu as pltpu
from jax.sharding import Mesh, PartitionSpec as P

D = 3584
TOPK = 8
EXP_DEV = 16
TOK = 128
EXPERTS = 256
BLOCKS = 28
CAP = 6
N_EXPERT = 16
SLOTS = N_EXPERT * CAP
FEAT = 56
CHUNKS = 4
WIDE = D // CHUNKS
PACKED = SLOTS * CHUNKS
META = 16
ROWS = SLOTS + META
PEERS = 16
SCALE = 2.5

ALL = ("yh", "x", "core", "z", "yl")
OWNERS = ("z", "yl")
NEAR = ("x", "core")
FAR = ("yh", "z", "yl")

f32 = jnp.float32
bf16 = jnp.bfloat16


def pack_matrix():
    rows = np.arange(PACKED)
    owner, rest = rows // (CHUNKS * CAP), rows % (CHUNKS * CAP)
    chunk, slot = rest // CAP, rest % CAP
    m = np.zeros((PACKED, PACKED), np.float32)
    m[rows, chunk * SLOTS + owner * CAP + slot] = 1
    return m


def stacked(v):
    return jnp.concatenate([v[:, c * WIDE : (c + 1) * WIDE] for c in range(CHUNKS)], axis=0)


def dot(a, b, **kw):
    return jnp.dot(a, b, preferred_element_type=f32, **kw)


def slot_matrix(lead, slots):
    pos = jnp.where(slots < CAP, (lead >> 4) * CAP + slots, 1000)
    rows = lax.broadcasted_iota(jnp.int32, (TOK, TOK), 0)
    return jnp.where(rows == pos, 1.0, 0.0)


def outgoing(idt_ref, slots_ref, tv_ref, bs_ref, eo_ref, pack_ref, out_ref, deq_ref):
    pick = slot_matrix(idt_ref[0:1, :], slots_ref[...]).astype(bf16)[:SLOTS]
    pack = pack_ref[...]
    out_ref[:, :WIDE] = dot(pack, stacked(eo_ref[...])).astype(bf16)
    scales = dot(pick, bs_ref[...]).astype(bf16)
    block = lax.broadcasted_iota(jnp.int32, (BLOCKS, D), 0)
    lane = lax.broadcasted_iota(jnp.int32, (BLOCKS, D), 1)
    spread = jnp.where((lane >> 7) == block, 1.0, 0.0).astype(bf16)
    deq = (dot(pick, tv_ref[...]) * dot(scales, spread)).astype(bf16)
    deq_ref[...] = deq
    out_ref[:, WIDE:] = dot(pack, stacked(deq)).astype(bf16)


def prepare(idt_ref, slots_ref, ids_ref, logits_ref, og_ref, deq_ref, pack_ref, og_out, near_out):
    pick = slot_matrix(idt_ref[0:1, :], slots_ref[...]).astype(bf16)
    og = dot(pick[:SLOTS], og_ref[...]).astype(bf16)
    og_out[...] = dot(pack_ref[...], stacked(og)).astype(bf16)
    logits = logits_ref[...]
    ids = ids_ref[...]
    wide_lane = lax.broadcasted_iota(jnp.int32, (TOK, EXPERTS), 1)
    lane = lax.broadcasted_iota(jnp.int32, (TOK, TOK), 1)
    chosen = jnp.zeros((TOK, TOK), f32)
    idf = jnp.zeros((TOK, TOK), f32)
    for k in range(TOPK):
        idk = ids[:, k : k + 1]
        one = jnp.sum(jnp.where(wide_lane == idk, logits, 0.0), axis=1, keepdims=True)
        chosen = jnp.where(lane == k, one, chosen)
        idf = jnp.where(lane == k, idk.astype(f32), idf)
    a = 1.0 / (1.0 + jnp.exp(-chosen))
    total = jnp.sum(jnp.where(lane < TOPK, a, 0.0), axis=1, keepdims=True)
    lead = jnp.where(lane == 0, 1.0, 0.0)
    coef = SCALE * (lead - a[:, 0:1] / total) / total * a * (1.0 - a)
    coef = jnp.where(lane < TOPK, coef, 0.0)
    high = coef.astype(bf16).astype(f32)
    low = coef - high
    meta = idf + pltpu.roll(high, TOPK, 1) + pltpu.roll(low, 2 * TOPK, 1)
    meta = jnp.transpose(dot(pick, meta.astype(bf16)))
    top = jnp.concatenate([meta[0:8], meta[8:16]], axis=1)
    bottom = jnp.concatenate([meta[16:24], jnp.zeros((8, TOK), f32)], axis=1)
    block = jnp.concatenate([top, bottom], axis=0).astype(bf16)
    deq = deq_ref[...]
    gap = jnp.zeros((SLOTS, 64 - FEAT), bf16)
    for k in range(PEERS):
        parts = []
        for q in range(CHUNKS):
            at = q * WIDE + k * FEAT
            parts += [deq[:, at : at + FEAT], gap]
        near_out[k, :SLOTS, :] = jnp.concatenate(parts, axis=1)
        near_out[k, SLOTS:, :] = block


def gate(og_ref, got_ref, pack_ref, idt_ref, slots_ref, gate_ref, send_ref):
    prod = og_ref[...].astype(f32) * got_ref[:, :WIDE].astype(f32)
    part = prod[:, :TOK]
    for b in range(1, WIDE // TOK):
        part = part + prod[:, b * TOK : (b + 1) * TOK]
    pack = pack_ref[...].astype(f32)
    fold = pack[:, :SLOTS]
    for c in range(1, CHUNKS):
        fold = fold + pack[:, c * SLOTS : (c + 1) * SLOTS]
    fold = jnp.concatenate([fold, jnp.zeros((PACKED, TOK - SLOTS), f32)], axis=1)
    by_slot = lax.dot_general(
        part, fold, (((0,), (0,)), ((), ())), preferred_element_type=f32, precision=lax.Precision.HIGHEST
    )
    row = jnp.sum(by_slot, axis=0, keepdims=True)
    row = jnp.broadcast_to(row, (8, TOK))
    pick = slot_matrix(idt_ref[0:1, :], slots_ref[...])
    gate_ref[...] = dot(row, pick, precision=lax.Precision.HIGHEST)[0:1]
    send_ref[...] = jnp.broadcast_to(row[None], (PEERS, 8, TOK))


def unpack(got_ref, pack_ref, out_ref):
    got = got_ref[:, WIDE:]
    for c in range(CHUNKS):
        pick = pack_ref[:, c * SLOTS : (c + 1) * SLOTS]
        out_ref[:, c * WIDE : (c + 1) * WIDE] = lax.dot_general(
            pick, got, (((0,), (0,)), ((), ())), preferred_element_type=f32
        ).astype(bf16)


def expand(near_ref, out_ref):
    rows = lax.broadcasted_iota(jnp.int32, (EXPERTS, TOK), 0).astype(f32)
    for s in range(PEERS):
        meta = near_ref[s, SLOTS:, :].astype(f32)
        acc = jnp.zeros((EXPERTS, TOK), f32)
        for k in range(TOPK):
            coef = meta[k : k + 1, TOK:] + meta[8 + k : 9 + k, :TOK]
            acc = acc + jnp.where(rows == meta[k : k + 1, :TOK], coef, 0.0)
        out_ref[s] = acc


def contract(place_ref, near_ref, terms_ref, gg_ref, idt_ref, slots_ref, out_ref, acc_ref):
    yh, mine = place_ref[0], place_ref[1]
    for s in range(PEERS):
        left = (terms_ref[s] * gg_ref[s, 0:1, :]).astype(bf16)[:, :ROWS]
        part = dot(left, near_ref[s])
        if s == 0:
            acc_ref[...] = part
        else:
            acc_ref[...] += part
    lane = lax.broadcasted_iota(jnp.int32, (8, TOK), 1)
    row = lax.broadcasted_iota(jnp.int32, (8, TOK), 0)
    lead = idt_ref[0:1, :]
    pos = jnp.where(slots_ref[...] < CAP, (lead >> 4) * 8 + slots_ref[...], 1000)
    number = jnp.broadcast_to(((lead & 15) + 1).astype(f32), (8, TOK)).astype(bf16)
    srow = lax.broadcasted_iota(jnp.int32, (TOK, TOK), 0)
    place = jnp.where(srow == pos, 1.0, 0.0)
    named = jnp.sum(place * jnp.broadcast_to(((lead & 15) + 1).astype(f32), (TOK, TOK)), axis=1, keepdims=True)
    own_lane = jnp.where(mine < 8, FEAT + mine, 64 + FEAT + mine - 8)
    left_half = lane < 64
    for j in range(PEERS):
        tag = jnp.where(lane == own_lane, named[8 * j : 8 * j + 8], 0.0)
        for h in range(2):
            lo = acc_ref[16 * j : 16 * j + 8, TOK * h : TOK * (h + 1)]
            hi = acc_ref[16 * j + 8 : 16 * j + 16, TOK * h : TOK * (h + 1)]
            first = jnp.where(left_half, lo, pltpu.roll(hi, 64, 1))
            second = jnp.where(left_half, pltpu.roll(lo, 64, 1), hi)
            out_ref[(2 * h) * PEERS + j] = first + jnp.where(yh == 2 * h, tag, 0.0)
            out_ref[(2 * h + 1) * PEERS + j] = second + jnp.where(yh == 2 * h + 1, tag, 0.0)


def finish(far_ref, grad_ref, expert_ref):
    total = jnp.sum(far_ref[...], axis=0)
    grad_ref[0:8, :] = total[:, :FEAT]
    grad_ref[8:16, :] = total[:, 64 : 64 + FEAT]
    lane = lax.broadcasted_iota(jnp.int32, (TOK, TOK), 0)
    slot = lax.broadcasted_iota(jnp.int32, (TOK, TOK), 1)
    source = jnp.where(lane < 64, lane - FEAT, lane - 64 - FEAT + 8)
    tagged = ((lane >= FEAT) & (lane < 64)) | (lane >= 64 + FEAT)
    first = source * CAP
    hit = tagged & (slot >= first) & (slot < first + CAP)
    spread = dot(jnp.where(lax.broadcasted_iota(jnp.int32, (8, TOK), 1) % 64 >= FEAT, total, 0.0), jnp.where(hit, 1.0, 0.0), precision=lax.Precision.HIGHEST)
    row = lax.broadcasted_iota(jnp.int32, (8, TOK), 0)
    col = lax.broadcasted_iota(jnp.int32, (8, TOK), 1)
    value = jnp.sum(jnp.where(col % CAP == row, spread, 0.0), axis=0, keepdims=True)
    expert_ref[...] = (value[:, :SLOTS] + 0.5).astype(jnp.int32) - 1


def call(body, outs, args, flops=0, moved=0, scratch=(), scalars=0):
    specs = [pl.BlockSpec(memory_space=pltpu.SMEM)] * scalars
    specs += [pl.BlockSpec(memory_space=pltpu.VMEM)] * (len(args) - scalars)
    return pl.pallas_call(
        body,
        out_shape=[jax.ShapeDtypeStruct(s, t) for s, t in outs],
        in_specs=specs,
        out_specs=[pl.BlockSpec(memory_space=pltpu.VMEM)] * len(outs),
        scratch_shapes=list(scratch),
        compiler_params=pltpu.CompilerParams(vmem_limit_bytes=40 * 2**20),
        cost_estimate=pl.CostEstimate(flops=flops, bytes_accessed=moved, transcendentals=0),
        name=body.__name__,
    )(*args)


def swap(v, axes):
    return lax.all_to_all(v, axes, split_axis=0, concat_axis=0, tiled=True)


def shards(token_values, block_scales, route_ids, route_slots, router_logits, expert_outputs, output_grad):
    pack = jnp.asarray(pack_matrix(), bf16)
    idt = route_ids.T
    slots = route_slots.reshape(1, TOK)
    place = jnp.stack([lax.axis_index("yh"), lax.axis_index(OWNERS)]).astype(jnp.int32)
    out, deq = call(
        outgoing,
        [((PACKED, 2 * WIDE), bf16), ((SLOTS, D), bf16)],
        (idt, slots, token_values, block_scales, expert_outputs, pack),
    )
    got = swap(out, OWNERS)
    og, near = call(
        prepare,
        [((PACKED, WIDE), bf16), ((PEERS, ROWS, 256), bf16)],
        (idt, slots, route_ids, router_logits, output_grad, deq, pack),
    )
    near = swap(near, NEAR)
    (terms,) = call(expand, [((PEERS, EXPERTS, TOK), f32)], (near,))
    gates, send = call(
        gate, [((1, TOK), f32), ((PEERS, 8, TOK), f32)], (og, got, pack, idt, slots)
    )
    gg = swap(send, NEAR)
    (expert_inputs,) = call(unpack, [((SLOTS, D), bf16)], (got, pack))
    (far,) = call(
        contract,
        [((CHUNKS * PEERS, 8, TOK), f32)],
        (place, near, terms, gg, idt, slots),
        scratch=[pltpu.VMEM((EXPERTS, 256), f32)],
        scalars=1,
    )
    far = swap(far, FAR)
    grad, named = call(finish, [((EXP_DEV, FEAT), f32), ((1, SLOTS), jnp.int32)], (far,))
    return expert_inputs, named.reshape(SLOTS), gates.reshape(TOK), grad.T


def solution(mesh):
    fine = Mesh(mesh.devices.reshape(4, 8, 2, 8, 2), ALL)
    rows = P(ALL, None)
    return jax.shard_map(
        shards,
        mesh=fine,
        in_specs=(rows, rows, rows, P(ALL), rows, rows, rows),
        out_specs=(rows, P(ALL), P(ALL), P(("yh", "x", "core"), ("z", "yl"))),
        check_vma=False,
    )
```

```python
import jax
import jax.numpy as jnp
import numpy as np
from jax import lax
from jax.experimental import pallas as pl
from jax.experimental.pallas import tpu as pltpu
from jax.sharding import Mesh, PartitionSpec as P

D = 3584
TOPK = 8
EXP_DEV = 16
TOK = 128
EXPERTS = 256
BLOCKS = 28
CAP = 6
N_EXPERT = 16
SLOTS = N_EXPERT * CAP
FEAT = 56
CHUNKS = 4
WIDE = D // CHUNKS
PACKED = SLOTS * CHUNKS
META = 16
ROWS = SLOTS + META
PEERS = 16
RING = 8
STEPS = (0, 4, 3, 5, 2, 6, 1, 7)
HELD = 7
SCALE = 2.5

ALL = ("yh", "x", "core", "z", "yl")
OWNERS = ("z", "yl")
NEAR = ("x", "core")
FAR = ("yh", "z", "yl")

f32 = jnp.float32
bf16 = jnp.bfloat16


def pack_matrix():
    rows = np.arange(PACKED)
    owner, rest = rows // (CHUNKS * CAP), rows % (CHUNKS * CAP)
    chunk, slot = rest // CAP, rest % CAP
    m = np.zeros((PACKED, PACKED), np.float32)
    m[rows, chunk * SLOTS + owner * CAP + slot] = 1
    return m


def stacked(v):
    return jnp.concatenate([v[:, c * WIDE : (c + 1) * WIDE] for c in range(CHUNKS)], axis=0)


def dot(a, b, **kw):
    return jnp.dot(a, b, preferred_element_type=f32, **kw)


def slot_matrix(lead, slots):
    pos = jnp.where(slots < CAP, (lead >> 4) * CAP + slots, 1000)
    rows = lax.broadcasted_iota(jnp.int32, (TOK, TOK), 0)
    return jnp.where(rows == pos, 1.0, 0.0)


def outgoing(idt_hbm, slots_hbm, tv_hbm, bst_hbm, eo_hbm, pack_hbm, out_hbm, deq_hbm,
             idt_ref, slots_ref, tv_ref, bst_ref, eo_ref, pack_ref, back_ref, rows_ref, deq_ref, sems, out_sems):
    pairs = [
        (eo_hbm, eo_ref),
        (pack_hbm, pack_ref),
        (idt_hbm, idt_ref),
        (slots_hbm, slots_ref),
        (bst_hbm, bst_ref),
        (tv_hbm, tv_ref),
    ]
    copies = [pltpu.make_async_copy(a, b, sems.at[n]) for n, (a, b) in enumerate(pairs)]
    for c in copies:
        c.start()
    copies[0].wait()
    copies[1].wait()
    pack = pack_ref[...]
    back_ref[...] = dot(pack, stacked(eo_ref[...])).astype(bf16)
    back_out = pltpu.make_async_copy(back_ref, out_hbm.at[:, pl.ds(0, WIDE)], out_sems.at[0])
    back_out.start()
    for c in copies[2:]:
        c.wait()
    pick = slot_matrix(idt_ref[0:1, :], slots_ref[...]).astype(bf16)[:SLOTS]
    scales = lax.dot_general(
        pick, bst_ref[...], (((1,), (1,)), ((), ())), preferred_element_type=f32
    ).astype(bf16)
    block = lax.broadcasted_iota(jnp.int32, (BLOCKS, D), 0)
    lane = lax.broadcasted_iota(jnp.int32, (BLOCKS, D), 1)
    spread = jnp.where((lane >> 7) == block, 1.0, 0.0).astype(bf16)
    deq = (dot(pick, tv_ref[...]) * dot(scales, spread)).astype(bf16)
    deq_ref[...] = deq
    deq_out = pltpu.make_async_copy(deq_ref, deq_hbm, out_sems.at[2])
    deq_out.start()
    rows_ref[...] = dot(pack, stacked(deq)).astype(bf16)
    rows_out = pltpu.make_async_copy(rows_ref, out_hbm.at[:, pl.ds(WIDE, WIDE)], out_sems.at[1])
    rows_out.start()
    deq_out.wait()
    back_out.wait()
    rows_out.wait()


def prepare(place_ref, idt_ref, slots_ref, ids_ref, logits_ref, og_ref, deq_ref, pack_ref, og_hbm, own_out, other_out, og_out, og_sem):
    pick = slot_matrix(idt_ref[0:1, :], slots_ref[...]).astype(bf16)
    og = dot(pick[:SLOTS], og_ref[...]).astype(bf16)
    og_out[...] = dot(pack_ref[...], stacked(og)).astype(bf16)
    og_copy = pltpu.make_async_copy(og_out, og_hbm, og_sem)
    og_copy.start()
    logits = logits_ref[...]
    ids = ids_ref[...]
    wide_lane = lax.broadcasted_iota(jnp.int32, (TOK, EXPERTS), 1)
    lane = lax.broadcasted_iota(jnp.int32, (TOK, TOK), 1)
    chosen = jnp.zeros((TOK, TOK), f32)
    idf = jnp.zeros((TOK, TOK), f32)
    for k in range(TOPK):
        idk = ids[:, k : k + 1]
        one = jnp.sum(jnp.where(wide_lane == idk, logits, 0.0), axis=1, keepdims=True)
        chosen = jnp.where(lane == k, one, chosen)
        idf = jnp.where(lane == k, idk.astype(f32), idf)
    a = 1.0 / (1.0 + jnp.exp(-chosen))
    total = jnp.sum(jnp.where(lane < TOPK, a, 0.0), axis=1, keepdims=True)
    lead = jnp.where(lane == 0, 1.0, 0.0)
    coef = SCALE * (lead - a[:, 0:1] / total) / total * a * (1.0 - a)
    coef = jnp.where(lane < TOPK, coef, 0.0)
    high = coef.astype(bf16).astype(f32)
    low = coef - high
    meta = idf + pltpu.roll(high, TOPK, 1) + pltpu.roll(low, 2 * TOPK, 1)
    meta = jnp.transpose(dot(pick, meta.astype(bf16)))
    top = jnp.concatenate([meta[0:8], meta[8:16]], axis=1)
    bottom = jnp.concatenate([meta[16:24], jnp.zeros((8, TOK), f32)], axis=1)
    block = jnp.concatenate([top, bottom], axis=0).astype(bf16)
    deq = deq_ref[...]
    gap = jnp.zeros((SLOTS, 64 - FEAT), bf16)
    x, core = place_ref[2], place_ref[3]
    for far_x in range(RING):
        step = (far_x - x) & (RING - 1)
        pieces = []
        for k in (2 * far_x, 2 * far_x + 1):
            parts = []
            for q in range(CHUNKS):
                at = q * WIDE + k * FEAT
                parts += [deq[:, at : at + FEAT], gap]
            pieces.append(jnp.concatenate(parts, axis=1))
        own_out[step, :SLOTS, :] = jnp.where(core == 0, pieces[0], pieces[1])
        other_out[step, :SLOTS, :] = jnp.where(core == 0, pieces[1], pieces[0])
        own_out[step, SLOTS:, :] = block
        other_out[step, SLOTS:, :] = block
    og_copy.wait()


def join(own_ref, other_ref, *outs):
    for step in range(RING):
        outs[step][:ROWS, :] = own_ref[step]
        outs[step][ROWS:, :] = other_ref[step]


def gate(og_ref, got_ref, pack_ref, idt_ref, slots_ref, gate_ref, send_ref):
    prod = og_ref[...].astype(f32) * got_ref[:, :WIDE].astype(f32)
    part = prod[:, :TOK]
    for b in range(1, WIDE // TOK):
        part = part + prod[:, b * TOK : (b + 1) * TOK]
    pack = pack_ref[...].astype(f32)
    fold = pack[:, :SLOTS]
    for c in range(1, CHUNKS):
        fold = fold + pack[:, c * SLOTS : (c + 1) * SLOTS]
    fold = jnp.concatenate([fold, jnp.zeros((PACKED, TOK - SLOTS), f32)], axis=1)
    by_slot = lax.dot_general(
        part, fold, (((0,), (0,)), ((), ())), preferred_element_type=f32, precision=lax.Precision.HIGHEST
    )
    row = jnp.sum(by_slot, axis=0, keepdims=True)
    row = jnp.broadcast_to(row, (8, TOK))
    pick = slot_matrix(idt_ref[0:1, :], slots_ref[...])
    gate_ref[...] = dot(row, pick, precision=lax.Precision.HIGHEST)[0:1]
    send_ref[...] = jnp.broadcast_to(row[None], (PEERS, 8, TOK))


def unpack(got_ref, pack_ref, out_ref):
    got = got_ref[:, WIDE:]
    for c in range(CHUNKS):
        pick = pack_ref[:, c * SLOTS : (c + 1) * SLOTS]
        out_ref[:, c * WIDE : (c + 1) * WIDE] = lax.dot_general(
            pick, got, (((0,), (0,)), ((), ())), preferred_element_type=f32
        ).astype(bf16)


def contract(place_ref, gg_ref, idt_ref, slots_ref, *refs):
    near_refs = refs[:RING]
    out_hbm, acc_ref, out_ref, out_sem = refs[RING:]
    yh, mine, x, core = (place_ref[n] for n in range(4))
    rows = lax.broadcasted_iota(jnp.int32, (EXPERTS, TOK), 0).astype(f32)
    for n, step in enumerate(STEPS):
        left = []
        for o in range(2):
            at = o * ROWS + SLOTS
            meta = near_refs[n][at : at + META, :].astype(f32)
            source = ((x - step) & (RING - 1)) * 2 + (core ^ o)
            term = jnp.zeros((EXPERTS, TOK), f32)
            for k in range(TOPK):
                coef = meta[k : k + 1, TOK:] + meta[8 + k : 9 + k, :TOK]
                term = term + jnp.where(rows == meta[k : k + 1, :TOK], coef * gg_ref[source, 0:1, :], 0.0)
            left.append(term.astype(bf16)[:, :ROWS])
        part = dot(jnp.concatenate(left, axis=1), near_refs[n][...])
        if n == 0:
            acc_ref[...] = part
        else:
            acc_ref[...] += part
    lane = lax.broadcasted_iota(jnp.int32, (8, TOK), 1)
    row = lax.broadcasted_iota(jnp.int32, (8, TOK), 0)
    lead = idt_ref[0:1, :]
    pos = jnp.where(slots_ref[...] < CAP, (lead >> 4) * 8 + slots_ref[...], 1000)
    srow = lax.broadcasted_iota(jnp.int32, (TOK, TOK), 0)
    place = jnp.where(srow == pos, 1.0, 0.0)
    named = jnp.sum(place * jnp.broadcast_to(((lead & 15) + 1).astype(f32), (TOK, TOK)), axis=1, keepdims=True)
    own_lane = jnp.where(mine < 8, FEAT + mine, 64 + FEAT + mine - 8)
    left_half = lane < 64
    for j in range(PEERS):
        tag = jnp.where(lane == own_lane, named[8 * j : 8 * j + 8], 0.0)
        for h in range(2):
            lo = acc_ref[16 * j : 16 * j + 8, TOK * h : TOK * (h + 1)]
            hi = acc_ref[16 * j + 8 : 16 * j + 16, TOK * h : TOK * (h + 1)]
            first = jnp.where(left_half, lo, pltpu.roll(hi, 64, 1))
            second = jnp.where(left_half, pltpu.roll(lo, 64, 1), hi)
            out_ref[(2 * h) * PEERS + j] = (first + jnp.where(yh == 2 * h, tag, 0.0)).astype(bf16)
            out_ref[(2 * h + 1) * PEERS + j] = (second + jnp.where(yh == 2 * h + 1, tag, 0.0)).astype(bf16)

    out_copy = pltpu.make_async_copy(out_ref, out_hbm, out_sem)
    out_copy.start()
    out_copy.wait()

def finish(far_ref, grad_ref, expert_ref):
    total = jnp.sum(far_ref[...].astype(f32), axis=0)
    grad_ref[0:8, :] = total[:, :FEAT]
    grad_ref[8:16, :] = total[:, 64 : 64 + FEAT]
    lane = lax.broadcasted_iota(jnp.int32, (TOK, TOK), 0)
    slot = lax.broadcasted_iota(jnp.int32, (TOK, TOK), 1)
    source = jnp.where(lane < 64, lane - FEAT, lane - 64 - FEAT + 8)
    tagged = ((lane >= FEAT) & (lane < 64)) | (lane >= 64 + FEAT)
    first = source * CAP
    hit = tagged & (slot >= first) & (slot < first + CAP)
    spread = dot(jnp.where(lax.broadcasted_iota(jnp.int32, (8, TOK), 1) % 64 >= FEAT, total, 0.0), jnp.where(hit, 1.0, 0.0), precision=lax.Precision.HIGHEST)
    row = lax.broadcasted_iota(jnp.int32, (8, TOK), 0)
    col = lax.broadcasted_iota(jnp.int32, (8, TOK), 1)
    value = jnp.sum(jnp.where(col % CAP == row, spread, 0.0), axis=0, keepdims=True)
    expert_ref[...] = (value[:, :SLOTS] + 0.5).astype(jnp.int32) - 1


def call(body, outs, args, scratch=(), scalars=0, hbm_in=False, hbm_last=0, hbm_out=(), limit=32):
    vmem, hbm = pl.BlockSpec(memory_space=pltpu.VMEM), pl.BlockSpec(memory_space=pl.ANY)
    specs = [pl.BlockSpec(memory_space=pltpu.SMEM)] * scalars
    specs += [hbm if hbm_in else vmem] * (len(args) - scalars)
    specs[len(specs) - hbm_last :] = [hbm] * hbm_last
    return pl.pallas_call(
        body,
        out_shape=[jax.ShapeDtypeStruct(s, t) for s, t in outs],
        in_specs=specs,
        out_specs=[hbm if n in hbm_out else vmem for n in range(len(outs))],
        scratch_shapes=list(scratch),
        compiler_params=pltpu.CompilerParams(vmem_limit_bytes=limit * 2**20),
        name=body.__name__,
    )(*args)


def swap(v, axes):
    return lax.all_to_all(v, axes, split_axis=0, concat_axis=0, tiled=True)


def shards(token_values, block_scales, route_ids, route_slots, router_logits, expert_outputs, output_grad):
    pack = jnp.asarray(pack_matrix(), bf16)
    idt = route_ids.T
    slots = route_slots.reshape(1, TOK)
    place = jnp.stack(
        [lax.axis_index("yh"), lax.axis_index(OWNERS), lax.axis_index("x"), lax.axis_index("core")]
    ).astype(jnp.int32)
    out, deq = call(
        outgoing,
        [((PACKED, 2 * WIDE), bf16), ((SLOTS, D), bf16)],
        (idt, slots, token_values, block_scales.T, expert_outputs, pack),
        scratch=[
            pltpu.VMEM((TOPK, TOK), jnp.int32),
            pltpu.VMEM((1, TOK), jnp.int32),
            pltpu.VMEM((TOK, D), bf16),
            pltpu.VMEM((BLOCKS, TOK), bf16),
            pltpu.VMEM((SLOTS, D), bf16),
            pltpu.VMEM((PACKED, PACKED), bf16),
            pltpu.VMEM((PACKED, WIDE), bf16),
            pltpu.VMEM((PACKED, WIDE), bf16),
            pltpu.VMEM((SLOTS, D), bf16),
            pltpu.SemaphoreType.DMA((6,)),
            pltpu.SemaphoreType.DMA((3,)),
        ],
        hbm_in=True,
        hbm_out=(0, 1),
        limit=58,
    )
    got = swap(out, OWNERS)
    og, own, other = call(
        prepare,
        [((PACKED, WIDE), bf16), ((RING, ROWS, 256), bf16), ((RING, ROWS, 256), bf16)],
        (place, idt, slots, route_ids, router_logits, output_grad, deq, pack),
        scratch=[pltpu.VMEM((PACKED, WIDE), bf16), pltpu.SemaphoreType.DMA],
        scalars=1,
        hbm_out=(0,),
    )
    other = lax.ppermute(other, "core", [(0, 1), (1, 0)])
    joined = call(join, [((2 * ROWS, 256), bf16)] * RING, (own, other))
    near = [joined[0]]
    for step in STEPS[1:]:
        near.append(lax.ppermute(joined[step], "x", [(i, (i + step) % RING) for i in range(RING)]))
    got, og, *near[:HELD] = lax.optimization_barrier((got, og, *near[:HELD]))
    gates, send = call(
        gate, [((1, TOK), f32), ((PEERS, 8, TOK), f32)], (og, got, pack, idt, slots)
    )
    gg = swap(send, NEAR)
    (expert_inputs,) = call(unpack, [((SLOTS, D), bf16)], (got, pack))
    (far,) = call(
        contract,
        [((CHUNKS * PEERS, 8, TOK), bf16)],
        (place, gg, idt, slots, *near),
        scratch=[
            pltpu.VMEM((EXPERTS, 256), f32),
            pltpu.VMEM((CHUNKS * PEERS, 8, TOK), bf16),
            pltpu.SemaphoreType.DMA,
        ],
        scalars=1,
        hbm_out=(0,),
        limit=32,
    )
    far = swap(far, FAR)
    grad, named = call(finish, [((EXP_DEV, FEAT), f32), ((1, SLOTS), jnp.int32)], (far,))
    return expert_inputs, named.reshape(SLOTS), gates.reshape(TOK), grad.T


def solution(mesh):
    fine = Mesh(mesh.devices.reshape(4, 8, 2, 8, 2), ALL)
    rows = P(ALL, None)
    return jax.shard_map(
        shards,
        mesh=fine,
        in_specs=(rows, rows, rows, P(ALL), rows, rows, rows),
        out_specs=(rows, P(ALL), P(ALL), P(("yh", "x", "core"), ("z", "yl"))),
        check_vma=False,
    )
```

```python
import jax
import jax.numpy as jnp
import numpy as np
from jax import lax
from jax.experimental import pallas as pl
from jax.experimental.pallas import tpu as pltpu
from jax.sharding import Mesh, PartitionSpec as P

D = 3584
TOPK = 8
EXP_DEV = 16
TOK = 128
EXPERTS = 256
BLOCKS = 28
CAP = 6
N_EXPERT = 16
SLOTS = N_EXPERT * CAP
FEAT = 56
CHUNKS = 4
WIDE = D // CHUNKS
PACKED = SLOTS * CHUNKS
META = 16
ROWS = SLOTS + META
PEERS = 16
RING = 8
STEPS = (0, 4, 3, 5, 2, 6, 1, 7)
HELD = 7
SCALE = 2.5

ALL = ("yh", "x", "core", "z", "yl")
OWNERS = ("z", "yl")
NEAR = ("x", "core")
FAR = ("yh", "z", "yl")

f32 = jnp.float32
bf16 = jnp.bfloat16


def pack_matrix():
    rows = np.arange(PACKED)
    owner, rest = rows // (CHUNKS * CAP), rows % (CHUNKS * CAP)
    chunk, slot = rest // CAP, rest % CAP
    m = np.zeros((PACKED, PACKED), np.float32)
    m[rows, chunk * SLOTS + owner * CAP + slot] = 1
    return m


def stacked(v):
    return jnp.concatenate([v[:, c * WIDE : (c + 1) * WIDE] for c in range(CHUNKS)], axis=0)


def dot(a, b, **kw):
    return jnp.dot(a, b, preferred_element_type=f32, **kw)


def slot_matrix(lead, slots):
    pos = jnp.where(slots < CAP, (lead >> 4) * CAP + slots, 1000)
    rows = lax.broadcasted_iota(jnp.int32, (TOK, TOK), 0)
    return jnp.where(rows == pos, 1.0, 0.0)


def outgoing(idt_hbm, slots_hbm, tv_hbm, bst_hbm, eo_hbm, pack_hbm, out_hbm, deq_hbm,
             idt_ref, slots_ref, tv_ref, bst_ref, eo_ref, pack_ref, back_ref, rows_ref, deq_ref, sems, out_sems):
    pairs = [
        (eo_hbm, eo_ref),
        (pack_hbm, pack_ref),
        (idt_hbm, idt_ref),
        (slots_hbm, slots_ref),
        (bst_hbm, bst_ref),
        (tv_hbm, tv_ref),
    ]
    copies = [pltpu.make_async_copy(a, b, sems.at[n]) for n, (a, b) in enumerate(pairs)]
    for c in copies:
        c.start()
    copies[0].wait()
    copies[1].wait()
    pack = pack_ref[...]
    back_ref[...] = dot(pack, stacked(eo_ref[...])).astype(bf16)
    back_out = pltpu.make_async_copy(back_ref, out_hbm.at[:, pl.ds(0, WIDE)], out_sems.at[0])
    back_out.start()
    for c in copies[2:]:
        c.wait()
    pick = slot_matrix(idt_ref[0:1, :], slots_ref[...]).astype(bf16)[:SLOTS]
    scales = lax.dot_general(
        pick, bst_ref[...], (((1,), (1,)), ((), ())), preferred_element_type=f32
    ).astype(bf16)
    block = lax.broadcasted_iota(jnp.int32, (BLOCKS, D), 0)
    lane = lax.broadcasted_iota(jnp.int32, (BLOCKS, D), 1)
    spread = jnp.where((lane >> 7) == block, 1.0, 0.0).astype(bf16)
    deq = (dot(pick, tv_ref[...]) * dot(scales, spread)).astype(bf16)
    deq_ref[...] = deq
    deq_out = pltpu.make_async_copy(deq_ref, deq_hbm, out_sems.at[2])
    deq_out.start()
    rows_ref[...] = dot(pack, stacked(deq)).astype(bf16)
    rows_out = pltpu.make_async_copy(rows_ref, out_hbm.at[:, pl.ds(WIDE, WIDE)], out_sems.at[1])
    rows_out.start()
    deq_out.wait()
    back_out.wait()
    rows_out.wait()


def grads(idt_ref, slots_ref, og_ref, pack_ref, og_out):
    pick = slot_matrix(idt_ref[0:1, :], slots_ref[...]).astype(bf16)
    og = dot(pick[:SLOTS], og_ref[...]).astype(bf16)
    og_out[...] = dot(pack_ref[...], stacked(og)).astype(bf16)


def prepare(place_ref, idt_ref, slots_ref, ids_ref, logits_ref, deq_ref, own_out, other_out):
    pick = slot_matrix(idt_ref[0:1, :], slots_ref[...]).astype(bf16)
    logits = logits_ref[...]
    ids = ids_ref[...]
    wide_lane = lax.broadcasted_iota(jnp.int32, (TOK, EXPERTS), 1)
    lane = lax.broadcasted_iota(jnp.int32, (TOK, TOK), 1)
    chosen = jnp.zeros((TOK, TOK), f32)
    idf = jnp.zeros((TOK, TOK), f32)
    for k in range(TOPK):
        idk = ids[:, k : k + 1]
        one = jnp.sum(jnp.where(wide_lane == idk, logits, 0.0), axis=1, keepdims=True)
        chosen = jnp.where(lane == k, one, chosen)
        idf = jnp.where(lane == k, idk.astype(f32), idf)
    a = 1.0 / (1.0 + jnp.exp(-chosen))
    total = jnp.sum(jnp.where(lane < TOPK, a, 0.0), axis=1, keepdims=True)
    lead = jnp.where(lane == 0, 1.0, 0.0)
    coef = SCALE * (lead - a[:, 0:1] / total) / total * a * (1.0 - a)
    coef = jnp.where(lane < TOPK, coef, 0.0)
    high = coef.astype(bf16).astype(f32)
    low = coef - high
    meta = idf + pltpu.roll(high, TOPK, 1) + pltpu.roll(low, 2 * TOPK, 1)
    meta = jnp.transpose(dot(pick, meta.astype(bf16)))
    top = jnp.concatenate([meta[0:8], meta[8:16]], axis=1)
    bottom = jnp.concatenate([meta[16:24], jnp.zeros((8, TOK), f32)], axis=1)
    block = jnp.concatenate([top, bottom], axis=0).astype(bf16)
    deq = deq_ref[...]
    gap = jnp.zeros((SLOTS, 64 - FEAT), bf16)
    x, core = place_ref[2], place_ref[3]
    for far_x in range(RING):
        step = (far_x - x) & (RING - 1)
        pieces = []
        for k in (2 * far_x, 2 * far_x + 1):
            parts = []
            for q in range(CHUNKS):
                at = q * WIDE + k * FEAT
                parts += [deq[:, at : at + FEAT], gap]
            pieces.append(jnp.concatenate(parts, axis=1))
        own_out[step, :SLOTS, :] = jnp.where(core == 0, pieces[0], pieces[1])
        other_out[step, :SLOTS, :] = jnp.where(core == 0, pieces[1], pieces[0])
        own_out[step, SLOTS:, :] = block
        other_out[step, SLOTS:, :] = block


def join(own_ref, other_ref, *outs):
    for step in range(RING):
        outs[step][:ROWS, :] = own_ref[step]
        outs[step][ROWS:, :] = other_ref[step]


def gate(og_ref, got_ref, pack_ref, idt_ref, slots_ref, gate_ref, send_ref):
    prod = og_ref[...].astype(f32) * got_ref[:, :WIDE].astype(f32)
    part = prod[:, :TOK]
    for b in range(1, WIDE // TOK):
        part = part + prod[:, b * TOK : (b + 1) * TOK]
    pack = pack_ref[...].astype(f32)
    fold = pack[:, :SLOTS]
    for c in range(1, CHUNKS):
        fold = fold + pack[:, c * SLOTS : (c + 1) * SLOTS]
    fold = jnp.concatenate([fold, jnp.zeros((PACKED, TOK - SLOTS), f32)], axis=1)
    by_slot = lax.dot_general(
        part, fold, (((0,), (0,)), ((), ())), preferred_element_type=f32, precision=lax.Precision.HIGHEST
    )
    row = jnp.sum(by_slot, axis=0, keepdims=True)
    row = jnp.broadcast_to(row, (8, TOK))
    pick = slot_matrix(idt_ref[0:1, :], slots_ref[...])
    gate_ref[...] = dot(row, pick, precision=lax.Precision.HIGHEST)[0:1]
    send_ref[...] = jnp.broadcast_to(row[None], (PEERS, 8, TOK))


def unpack(got_ref, pack_ref, out_ref):
    got = got_ref[:, WIDE:]
    for c in range(CHUNKS):
        pick = pack_ref[:, c * SLOTS : (c + 1) * SLOTS]
        out_ref[:, c * WIDE : (c + 1) * WIDE] = lax.dot_general(
            pick, got, (((0,), (0,)), ((), ())), preferred_element_type=f32
        ).astype(bf16)


def contract(place_ref, gg_ref, idt_ref, slots_ref, *refs):
    near_refs = refs[:RING]
    out_hbm, acc_ref, out_ref, out_sem = refs[RING:]
    yh, mine, x, core = (place_ref[n] for n in range(4))
    rows = lax.broadcasted_iota(jnp.int32, (EXPERTS, TOK), 0).astype(f32).astype(bf16)
    for n, step in enumerate(STEPS):
        left = []
        for o in range(2):
            at = o * ROWS + SLOTS
            meta = near_refs[n][at : at + META, :].astype(f32)
            source = ((x - step) & (RING - 1)) * 2 + (core ^ o)
            term = jnp.zeros((EXPERTS, TOK), bf16)
            for k in range(TOPK):
                coef = meta[k : k + 1, TOK:] + meta[8 + k : 9 + k, :TOK]
                value = (coef * gg_ref[source, 0:1, :]).astype(bf16)
                term = jnp.where(rows == meta[k : k + 1, :TOK].astype(bf16), value, term)
            left.append(term[:, :ROWS])
        part = dot(jnp.concatenate(left, axis=1), near_refs[n][...])
        if n == 0:
            acc_ref[...] = part
        else:
            acc_ref[...] += part
    lane = lax.broadcasted_iota(jnp.int32, (8, TOK), 1)
    row = lax.broadcasted_iota(jnp.int32, (8, TOK), 0)
    lead = idt_ref[0:1, :]
    pos = jnp.where(slots_ref[...] < CAP, (lead >> 4) * 8 + slots_ref[...], 1000)
    srow = lax.broadcasted_iota(jnp.int32, (TOK, TOK), 0)
    place = jnp.where(srow == pos, 1.0, 0.0)
    named = jnp.sum(place * jnp.broadcast_to(((lead & 15) + 1).astype(f32), (TOK, TOK)), axis=1, keepdims=True)
    own_lane = jnp.where(mine < 8, FEAT + mine, 64 + FEAT + mine - 8)
    left_half = lane < 64
    for j in range(PEERS):
        tag = jnp.where(lane == own_lane, named[8 * j : 8 * j + 8], 0.0)
        for h in range(2):
            lo = acc_ref[16 * j : 16 * j + 8, TOK * h : TOK * (h + 1)]
            hi = acc_ref[16 * j + 8 : 16 * j + 16, TOK * h : TOK * (h + 1)]
            first = jnp.where(left_half, lo, pltpu.roll(hi, 64, 1))
            second = jnp.where(left_half, pltpu.roll(lo, 64, 1), hi)
            out_ref[(2 * h) * PEERS + j] = (first + jnp.where(yh == 2 * h, tag, 0.0)).astype(bf16)
            out_ref[(2 * h + 1) * PEERS + j] = (second + jnp.where(yh == 2 * h + 1, tag, 0.0)).astype(bf16)

    out_copy = pltpu.make_async_copy(out_ref, out_hbm, out_sem)
    out_copy.start()
    out_copy.wait()

def finish(far_ref, grad_ref, expert_ref):
    total = jnp.sum(far_ref[...].astype(f32), axis=0)
    grad_ref[0:8, :] = total[:, :FEAT]
    grad_ref[8:16, :] = total[:, 64 : 64 + FEAT]
    lane = lax.broadcasted_iota(jnp.int32, (TOK, TOK), 0)
    slot = lax.broadcasted_iota(jnp.int32, (TOK, TOK), 1)
    source = jnp.where(lane < 64, lane - FEAT, lane - 64 - FEAT + 8)
    tagged = ((lane >= FEAT) & (lane < 64)) | (lane >= 64 + FEAT)
    first = source * CAP
    hit = tagged & (slot >= first) & (slot < first + CAP)
    spread = dot(jnp.where(lax.broadcasted_iota(jnp.int32, (8, TOK), 1) % 64 >= FEAT, total, 0.0), jnp.where(hit, 1.0, 0.0), precision=lax.Precision.HIGHEST)
    row = lax.broadcasted_iota(jnp.int32, (8, TOK), 0)
    col = lax.broadcasted_iota(jnp.int32, (8, TOK), 1)
    value = jnp.sum(jnp.where(col % CAP == row, spread, 0.0), axis=0, keepdims=True)
    expert_ref[...] = (value[:, :SLOTS] + 0.5).astype(jnp.int32) - 1


def call(body, outs, args, scratch=(), scalars=0, hbm_in=False, hbm_last=0, hbm_out=(), limit=32):
    vmem, hbm = pl.BlockSpec(memory_space=pltpu.VMEM), pl.BlockSpec(memory_space=pl.ANY)
    specs = [pl.BlockSpec(memory_space=pltpu.SMEM)] * scalars
    specs += [hbm if hbm_in else vmem] * (len(args) - scalars)
    specs[len(specs) - hbm_last :] = [hbm] * hbm_last
    return pl.pallas_call(
        body,
        out_shape=[jax.ShapeDtypeStruct(s, t) for s, t in outs],
        in_specs=specs,
        out_specs=[hbm if n in hbm_out else vmem for n in range(len(outs))],
        scratch_shapes=list(scratch),
        compiler_params=pltpu.CompilerParams(vmem_limit_bytes=limit * 2**20),
        name=body.__name__,
    )(*args)


def swap(v, axes):
    return lax.all_to_all(v, axes, split_axis=0, concat_axis=0, tiled=True)


def shards(token_values, block_scales, route_ids, route_slots, router_logits, expert_outputs, output_grad):
    pack = jnp.asarray(pack_matrix(), bf16)
    idt = route_ids.T
    slots = route_slots.reshape(1, TOK)
    place = jnp.stack(
        [lax.axis_index("yh"), lax.axis_index(OWNERS), lax.axis_index("x"), lax.axis_index("core")]
    ).astype(jnp.int32)
    out, deq = call(
        outgoing,
        [((PACKED, 2 * WIDE), bf16), ((SLOTS, D), bf16)],
        (idt, slots, token_values, block_scales.T, expert_outputs, pack),
        scratch=[
            pltpu.VMEM((TOPK, TOK), jnp.int32),
            pltpu.VMEM((1, TOK), jnp.int32),
            pltpu.VMEM((TOK, D), bf16),
            pltpu.VMEM((BLOCKS, TOK), bf16),
            pltpu.VMEM((SLOTS, D), bf16),
            pltpu.VMEM((PACKED, PACKED), bf16),
            pltpu.VMEM((PACKED, WIDE), bf16),
            pltpu.VMEM((PACKED, WIDE), bf16),
            pltpu.VMEM((SLOTS, D), bf16),
            pltpu.SemaphoreType.DMA((6,)),
            pltpu.SemaphoreType.DMA((3,)),
        ],
        hbm_in=True,
        hbm_out=(0, 1),
        limit=58,
    )
    got = swap(out, OWNERS)
    own, other = call(
        prepare,
        [((RING, ROWS, 256), bf16), ((RING, ROWS, 256), bf16)],
        (place, idt, slots, route_ids, router_logits, deq),
        scalars=1,
    )
    own, other, output_grad = lax.optimization_barrier((own, other, output_grad))
    (og,) = call(grads, [((PACKED, WIDE), bf16)], (idt, slots, output_grad, pack))
    other = lax.ppermute(other, "core", [(0, 1), (1, 0)])
    other, og = lax.optimization_barrier((other, og))
    joined = call(join, [((2 * ROWS, 256), bf16)] * RING, (own, other))
    near = [joined[0]]
    for step in STEPS[1:]:
        near.append(lax.ppermute(joined[step], "x", [(i, (i + step) % RING) for i in range(RING)]))
    got, og, *near[:HELD] = lax.optimization_barrier((got, og, *near[:HELD]))
    gates, send = call(
        gate, [((1, TOK), f32), ((PEERS, 8, TOK), f32)], (og, got, pack, idt, slots)
    )
    gg = swap(send, NEAR)
    (expert_inputs,) = call(unpack, [((SLOTS, D), bf16)], (got, pack))
    (far,) = call(
        contract,
        [((CHUNKS * PEERS, 8, TOK), bf16)],
        (place, gg, idt, slots, *near),
        scratch=[
            pltpu.VMEM((EXPERTS, 256), f32),
            pltpu.VMEM((CHUNKS * PEERS, 8, TOK), bf16),
            pltpu.SemaphoreType.DMA,
        ],
        scalars=1,
        hbm_out=(0,),
        limit=32,
    )
    far = swap(far, FAR)
    grad, named = call(finish, [((EXP_DEV, FEAT), f32), ((1, SLOTS), jnp.int32)], (far,))
    return expert_inputs, named.reshape(SLOTS), gates.reshape(TOK), grad.T


def solution(mesh):
    fine = Mesh(mesh.devices.reshape(4, 8, 2, 8, 2), ALL)
    rows = P(ALL, None)
    return jax.shard_map(
        shards,
        mesh=fine,
        in_specs=(rows, rows, rows, P(ALL), rows, rows, rows),
        out_specs=(rows, P(ALL), P(ALL), P(("yh", "x", "core"), ("z", "yl"))),
        check_vma=False,
    )
```

```python
import jax
import jax.numpy as jnp
import numpy as np
from jax import lax
from jax.experimental import pallas as pl
from jax.experimental.pallas import tpu as pltpu
from jax.sharding import Mesh, PartitionSpec as P

D = 3584
TOPK = 8
EXP_DEV = 16
TOK = 128
EXPERTS = 256
BLOCKS = 28
CAP = 6
N_EXPERT = 16
SLOTS = N_EXPERT * CAP
FEAT = 56
CHUNKS = 4
WIDE = D // CHUNKS
PACKED = SLOTS * CHUNKS
META = 16
ROWS = SLOTS + META
PEERS = 16
RING = 8
STEPS = (0, 4, 3, 5, 2, 6, 1, 7)
HELD = 7
SCALE = 2.5

ALL = ("yh", "x", "core", "z", "yl")
OWNERS = ("z", "yl")
NEAR = ("x", "core")
FAR = ("yh", "z", "yl")

f32 = jnp.float32
bf16 = jnp.bfloat16


def pack_matrix():
    rows = np.arange(PACKED)
    owner, rest = rows // (CHUNKS * CAP), rows % (CHUNKS * CAP)
    chunk, slot = rest // CAP, rest % CAP
    m = np.zeros((PACKED, PACKED), np.float32)
    m[rows, chunk * SLOTS + owner * CAP + slot] = 1
    return m


def stacked(v):
    return jnp.concatenate([v[:, c * WIDE : (c + 1) * WIDE] for c in range(CHUNKS)], axis=0)


def dot(a, b, **kw):
    return jnp.dot(a, b, preferred_element_type=f32, **kw)


def slot_matrix(lead, slots):
    pos = jnp.where(slots < CAP, (lead >> 4) * CAP + slots, 1000)
    rows = lax.broadcasted_iota(jnp.int32, (TOK, TOK), 0)
    return jnp.where(rows == pos, 1.0, 0.0)


def outgoing(idt_hbm, slots_hbm, tv_hbm, bst_hbm, eo_hbm, pack_hbm, out_hbm, deq_hbm,
             idt_ref, slots_ref, tv_ref, bst_ref, eo_ref, pack_ref, back_ref, rows_ref, deq_ref, sems, out_sems):
    pairs = [
        (eo_hbm, eo_ref),
        (pack_hbm, pack_ref),
        (idt_hbm, idt_ref),
        (slots_hbm, slots_ref),
        (bst_hbm, bst_ref),
        (tv_hbm, tv_ref),
    ]
    copies = [pltpu.make_async_copy(a, b, sems.at[n]) for n, (a, b) in enumerate(pairs)]
    for c in copies:
        c.start()
    copies[0].wait()
    copies[1].wait()
    pack = pack_ref[...]
    back_ref[...] = dot(pack, stacked(eo_ref[...])).astype(bf16)
    back_out = pltpu.make_async_copy(back_ref, out_hbm.at[:, pl.ds(0, WIDE)], out_sems.at[0])
    back_out.start()
    for c in copies[2:]:
        c.wait()
    pick = slot_matrix(idt_ref[0:1, :], slots_ref[...]).astype(bf16)[:SLOTS]
    scales = lax.dot_general(
        pick, bst_ref[...], (((1,), (1,)), ((), ())), preferred_element_type=f32
    ).astype(bf16)
    block = lax.broadcasted_iota(jnp.int32, (BLOCKS, D), 0)
    lane = lax.broadcasted_iota(jnp.int32, (BLOCKS, D), 1)
    spread = jnp.where((lane >> 7) == block, 1.0, 0.0).astype(bf16)
    deq = (dot(pick, tv_ref[...]) * dot(scales, spread)).astype(bf16)
    deq_ref[...] = deq
    deq_out = pltpu.make_async_copy(deq_ref, deq_hbm, out_sems.at[2])
    deq_out.start()
    rows_ref[...] = dot(pack, stacked(deq)).astype(bf16)
    rows_out = pltpu.make_async_copy(rows_ref, out_hbm.at[:, pl.ds(WIDE, WIDE)], out_sems.at[1])
    rows_out.start()
    deq_out.wait()
    back_out.wait()
    rows_out.wait()


def grads(idt_ref, slots_ref, og_ref, pack_ref, og_out):
    pick = slot_matrix(idt_ref[0:1, :], slots_ref[...]).astype(bf16)
    og = dot(pick[:SLOTS], og_ref[...]).astype(bf16)
    og_out[...] = dot(pack_ref[...], stacked(og)).astype(bf16)


def prepare(place_ref, idt_ref, slots_ref, ids_ref, logits_ref, deq_ref, own_out, other_out):
    pick = slot_matrix(idt_ref[0:1, :], slots_ref[...]).astype(bf16)
    logits = logits_ref[...]
    ids = ids_ref[...]
    wide_lane = lax.broadcasted_iota(jnp.int32, (TOK, EXPERTS), 1)
    lane = lax.broadcasted_iota(jnp.int32, (TOK, TOK), 1)
    chosen = jnp.zeros((TOK, TOK), f32)
    idf = jnp.zeros((TOK, TOK), f32)
    for k in range(TOPK):
        idk = ids[:, k : k + 1]
        one = jnp.sum(jnp.where(wide_lane == idk, logits, 0.0), axis=1, keepdims=True)
        chosen = jnp.where(lane == k, one, chosen)
        idf = jnp.where(lane == k, idk.astype(f32), idf)
    a = 1.0 / (1.0 + jnp.exp(-chosen))
    total = jnp.sum(jnp.where(lane < TOPK, a, 0.0), axis=1, keepdims=True)
    lead = jnp.where(lane == 0, 1.0, 0.0)
    coef = SCALE * (lead - a[:, 0:1] / total) / total * a * (1.0 - a)
    coef = jnp.where(lane < TOPK, coef, 0.0)
    high = coef.astype(bf16).astype(f32)
    low = coef - high
    meta = idf + pltpu.roll(high, TOPK, 1) + pltpu.roll(low, 2 * TOPK, 1)
    meta = jnp.transpose(dot(pick, meta.astype(bf16)))
    top = jnp.concatenate([meta[0:8], meta[8:16]], axis=1)
    bottom = jnp.concatenate([meta[16:24], jnp.zeros((8, TOK), f32)], axis=1)
    block = jnp.concatenate([top, bottom], axis=0).astype(bf16)
    deq = deq_ref[...]
    gap = jnp.zeros((SLOTS, 64 - FEAT), bf16)
    x, core = place_ref[2], place_ref[3]
    for far_x in range(RING):
        step = (far_x - x) & (RING - 1)
        pieces = []
        for k in (2 * far_x, 2 * far_x + 1):
            parts = []
            for q in range(CHUNKS):
                at = q * WIDE + k * FEAT
                parts += [deq[:, at : at + FEAT], gap]
            pieces.append(jnp.concatenate(parts, axis=1))
        own_out[step, :SLOTS, :] = jnp.where(core == 0, pieces[0], pieces[1])
        other_out[step, :SLOTS, :] = jnp.where(core == 0, pieces[1], pieces[0])
        own_out[step, SLOTS:, :] = block
        other_out[step, SLOTS:, :] = block


def join(own_ref, other_ref, *outs):
    for step in range(RING):
        outs[step][:ROWS, :] = own_ref[step]
        outs[step][ROWS:, :] = other_ref[step]


def gate(og_ref, got_ref, pack_ref, idt_ref, slots_ref, gate_ref, send_ref):
    prod = og_ref[...].astype(f32) * got_ref[:, :WIDE].astype(f32)
    part = prod[:, :TOK]
    for b in range(1, WIDE // TOK):
        part = part + prod[:, b * TOK : (b + 1) * TOK]
    pack = pack_ref[...].astype(f32)
    fold = pack[:, :SLOTS]
    for c in range(1, CHUNKS):
        fold = fold + pack[:, c * SLOTS : (c + 1) * SLOTS]
    fold = jnp.concatenate([fold, jnp.zeros((PACKED, TOK - SLOTS), f32)], axis=1)
    by_slot = lax.dot_general(
        part, fold, (((0,), (0,)), ((), ())), preferred_element_type=f32, precision=lax.Precision.HIGHEST
    )
    row = jnp.sum(by_slot, axis=0, keepdims=True)
    row = jnp.broadcast_to(row, (8, TOK))
    pick = slot_matrix(idt_ref[0:1, :], slots_ref[...])
    gate_ref[...] = dot(row, pick, precision=lax.Precision.HIGHEST)[0:1]
    send_ref[...] = jnp.broadcast_to(row[None, 0:1], (PEERS, 1, TOK))


def unpack(got_ref, pack_ref, out_ref):
    got = got_ref[:, WIDE:]
    for c in range(CHUNKS):
        pick = pack_ref[:, c * SLOTS : (c + 1) * SLOTS]
        out_ref[:, c * WIDE : (c + 1) * WIDE] = lax.dot_general(
            pick, got, (((0,), (0,)), ((), ())), preferred_element_type=f32
        ).astype(bf16)


def contract(place_ref, gg_ref, idt_ref, slots_ref, *refs):
    near_refs = refs[:RING]
    out_hbm, acc_ref, out_ref, out_sem = refs[RING:]
    yh, mine, x, core = (place_ref[n] for n in range(4))
    rows = lax.broadcasted_iota(jnp.int32, (EXPERTS, TOK), 0).astype(f32).astype(bf16)
    for n, step in enumerate(STEPS):
        left = []
        for o in range(2):
            at = o * ROWS + SLOTS
            meta = near_refs[n][at : at + META, :].astype(f32)
            source = ((x - step) & (RING - 1)) * 2 + (core ^ o)
            term = jnp.zeros((EXPERTS, TOK), bf16)
            for k in range(TOPK):
                coef = meta[k : k + 1, TOK:] + meta[8 + k : 9 + k, :TOK]
                value = (coef * gg_ref[source, 0:1, :]).astype(bf16)
                term = jnp.where(rows == meta[k : k + 1, :TOK].astype(bf16), value, term)
            left.append(term[:, :ROWS])
        part = dot(jnp.concatenate(left, axis=1), near_refs[n][...])
        if n == 0:
            acc_ref[...] = part
        else:
            acc_ref[...] += part
    lane = lax.broadcasted_iota(jnp.int32, (8, TOK), 1)
    row = lax.broadcasted_iota(jnp.int32, (8, TOK), 0)
    lead = idt_ref[0:1, :]
    pos = jnp.where(slots_ref[...] < CAP, (lead >> 4) * 8 + slots_ref[...], 1000)
    srow = lax.broadcasted_iota(jnp.int32, (TOK, TOK), 0)
    place = jnp.where(srow == pos, 1.0, 0.0)
    named = jnp.sum(place * jnp.broadcast_to(((lead & 15) + 1).astype(f32), (TOK, TOK)), axis=1, keepdims=True)
    own_lane = jnp.where(mine < 8, FEAT + mine, 64 + FEAT + mine - 8)
    left_half = lane < 64
    for j in range(PEERS):
        tag = jnp.where(lane == own_lane, named[8 * j : 8 * j + 8], 0.0)
        for h in range(2):
            lo = acc_ref[16 * j : 16 * j + 8, TOK * h : TOK * (h + 1)]
            hi = acc_ref[16 * j + 8 : 16 * j + 16, TOK * h : TOK * (h + 1)]
            first = jnp.where(left_half, lo, pltpu.roll(hi, 64, 1))
            second = jnp.where(left_half, pltpu.roll(lo, 64, 1), hi)
            out_ref[(2 * h) * PEERS + j] = (first + jnp.where(yh == 2 * h, tag, 0.0)).astype(bf16)
            out_ref[(2 * h + 1) * PEERS + j] = (second + jnp.where(yh == 2 * h + 1, tag, 0.0)).astype(bf16)

    out_copy = pltpu.make_async_copy(out_ref, out_hbm, out_sem)
    out_copy.start()
    out_copy.wait()

def finish(far_ref, grad_ref, expert_ref):
    total = jnp.sum(far_ref[...].astype(f32), axis=0)
    grad_ref[0:8, :] = total[:, :FEAT]
    grad_ref[8:16, :] = total[:, 64 : 64 + FEAT]
    lane = lax.broadcasted_iota(jnp.int32, (TOK, TOK), 0)
    slot = lax.broadcasted_iota(jnp.int32, (TOK, TOK), 1)
    source = jnp.where(lane < 64, lane - FEAT, lane - 64 - FEAT + 8)
    tagged = ((lane >= FEAT) & (lane < 64)) | (lane >= 64 + FEAT)
    first = source * CAP
    hit = tagged & (slot >= first) & (slot < first + CAP)
    spread = dot(jnp.where(lax.broadcasted_iota(jnp.int32, (8, TOK), 1) % 64 >= FEAT, total, 0.0), jnp.where(hit, 1.0, 0.0), precision=lax.Precision.HIGHEST)
    row = lax.broadcasted_iota(jnp.int32, (8, TOK), 0)
    col = lax.broadcasted_iota(jnp.int32, (8, TOK), 1)
    value = jnp.sum(jnp.where(col % CAP == row, spread, 0.0), axis=0, keepdims=True)
    expert_ref[...] = (value[:, :SLOTS] + 0.5).astype(jnp.int32) - 1


def call(body, outs, args, scratch=(), scalars=0, hbm_in=False, hbm_last=0, hbm_out=(), limit=32):
    vmem, hbm = pl.BlockSpec(memory_space=pltpu.VMEM), pl.BlockSpec(memory_space=pl.ANY)
    specs = [pl.BlockSpec(memory_space=pltpu.SMEM)] * scalars
    specs += [hbm if hbm_in else vmem] * (len(args) - scalars)
    specs[len(specs) - hbm_last :] = [hbm] * hbm_last
    return pl.pallas_call(
        body,
        out_shape=[jax.ShapeDtypeStruct(s, t) for s, t in outs],
        in_specs=specs,
        out_specs=[hbm if n in hbm_out else vmem for n in range(len(outs))],
        scratch_shapes=list(scratch),
        compiler_params=pltpu.CompilerParams(vmem_limit_bytes=limit * 2**20),
        name=body.__name__,
    )(*args)


def swap(v, axes):
    return lax.all_to_all(v, axes, split_axis=0, concat_axis=0, tiled=True)


def shards(token_values, block_scales, route_ids, route_slots, router_logits, expert_outputs, output_grad):
    pack = jnp.asarray(pack_matrix(), bf16)
    idt = route_ids.T
    slots = route_slots.reshape(1, TOK)
    place = jnp.stack(
        [lax.axis_index("yh"), lax.axis_index(OWNERS), lax.axis_index("x"), lax.axis_index("core")]
    ).astype(jnp.int32)
    out, deq = call(
        outgoing,
        [((PACKED, 2 * WIDE), bf16), ((SLOTS, D), bf16)],
        (idt, slots, token_values, block_scales.T, expert_outputs, pack),
        scratch=[
            pltpu.VMEM((TOPK, TOK), jnp.int32),
            pltpu.VMEM((1, TOK), jnp.int32),
            pltpu.VMEM((TOK, D), bf16),
            pltpu.VMEM((BLOCKS, TOK), bf16),
            pltpu.VMEM((SLOTS, D), bf16),
            pltpu.VMEM((PACKED, PACKED), bf16),
            pltpu.VMEM((PACKED, WIDE), bf16),
            pltpu.VMEM((PACKED, WIDE), bf16),
            pltpu.VMEM((SLOTS, D), bf16),
            pltpu.SemaphoreType.DMA((6,)),
            pltpu.SemaphoreType.DMA((3,)),
        ],
        hbm_in=True,
        hbm_out=(0, 1),
        limit=58,
    )
    got = swap(out, OWNERS)
    own, other = call(
        prepare,
        [((RING, ROWS, 256), bf16), ((RING, ROWS, 256), bf16)],
        (place, idt, slots, route_ids, router_logits, deq),
        scalars=1,
    )
    own, other, output_grad = lax.optimization_barrier((own, other, output_grad))
    (og,) = call(grads, [((PACKED, WIDE), bf16)], (idt, slots, output_grad, pack))
    other = lax.ppermute(other, "core", [(0, 1), (1, 0)])
    other, og = lax.optimization_barrier((other, og))
    joined = call(join, [((2 * ROWS, 256), bf16)] * RING, (own, other))
    near = [joined[0]]
    for step in STEPS[1:]:
        near.append(lax.ppermute(joined[step], "x", [(i, (i + step) % RING) for i in range(RING)]))
    got, og, *near[:HELD] = lax.optimization_barrier((got, og, *near[:HELD]))
    gates, send = call(
        gate, [((1, TOK), f32), ((PEERS, 1, TOK), f32)], (og, got, pack, idt, slots)
    )
    gg = swap(send, NEAR)
    (expert_inputs,) = call(unpack, [((SLOTS, D), bf16)], (got, pack))
    (far,) = call(
        contract,
        [((CHUNKS * PEERS, 8, TOK), bf16)],
        (place, gg, idt, slots, *near),
        scratch=[
            pltpu.VMEM((EXPERTS, 256), f32),
            pltpu.VMEM((CHUNKS * PEERS, 8, TOK), bf16),
            pltpu.SemaphoreType.DMA,
        ],
        scalars=1,
        hbm_out=(0,),
        limit=32,
    )
    far = swap(far, FAR)
    grad, named = call(finish, [((EXP_DEV, FEAT), f32), ((1, SLOTS), jnp.int32)], (far,))
    return expert_inputs, named.reshape(SLOTS), gates.reshape(TOK), grad.T


def solution(mesh):
    fine = Mesh(mesh.devices.reshape(4, 8, 2, 8, 2), ALL)
    rows = P(ALL, None)
    return jax.shard_map(
        shards,
        mesh=fine,
        in_specs=(rows, rows, rows, P(ALL), rows, rows, rows),
        out_specs=(rows, P(ALL), P(ALL), P(("yh", "x", "core"), ("z", "yl"))),
        check_vma=False,
    )
```

```python
import jax
import jax.numpy as jnp
import numpy as np
from jax import lax
from jax.experimental import pallas as pl
from jax.experimental.pallas import tpu as pltpu
from jax.sharding import Mesh, PartitionSpec as P

D = 3584
TOPK = 8
EXP_DEV = 16
TOK = 128
EXPERTS = 256
BLOCKS = 28
CAP = 6
N_EXPERT = 16
SLOTS = N_EXPERT * CAP
FEAT = 56
CHUNKS = 4
WIDE = D // CHUNKS
PACKED = SLOTS * CHUNKS
META = 16
ROWS = SLOTS + META
PEERS = 16
RING = 8
STEPS = (0, 4, 5, 3, 7, 6, 2, 1)
HELD = 7
SCALE = 2.5

ALL = ("yh", "x", "core", "z", "yl")
OWNERS = ("z", "yl")
NEAR = ("x", "core")
FAR = ("yh", "z", "yl")

f32 = jnp.float32
bf16 = jnp.bfloat16


def pack_matrix():
    rows = np.arange(PACKED)
    owner, rest = rows // (CHUNKS * CAP), rows % (CHUNKS * CAP)
    chunk, slot = rest // CAP, rest % CAP
    m = np.zeros((PACKED, PACKED), np.float32)
    m[rows, chunk * SLOTS + owner * CAP + slot] = 1
    return m


def stacked(v):
    return jnp.concatenate([v[:, c * WIDE : (c + 1) * WIDE] for c in range(CHUNKS)], axis=0)


def dot(a, b, **kw):
    return jnp.dot(a, b, preferred_element_type=f32, **kw)


def slot_matrix(lead, slots):
    pos = jnp.where(slots < CAP, (lead >> 4) * CAP + slots, 1000)
    rows = lax.broadcasted_iota(jnp.int32, (TOK, TOK), 0)
    return jnp.where(rows == pos, 1.0, 0.0)


def outgoing(idt_hbm, slots_hbm, tv_hbm, bst_hbm, eo_hbm, pack_hbm, out_hbm, deq_hbm,
             idt_ref, slots_ref, tv_ref, bst_ref, eo_ref, pack_ref, back_ref, rows_ref, deq_ref, sems, out_sems):
    pairs = [
        (eo_hbm, eo_ref),
        (pack_hbm, pack_ref),
        (idt_hbm, idt_ref),
        (slots_hbm, slots_ref),
        (bst_hbm, bst_ref),
        (tv_hbm, tv_ref),
    ]
    copies = [pltpu.make_async_copy(a, b, sems.at[n]) for n, (a, b) in enumerate(pairs)]
    for c in copies:
        c.start()
    copies[0].wait()
    copies[1].wait()
    pack = pack_ref[...]
    back_ref[...] = dot(pack, stacked(eo_ref[...])).astype(bf16)
    back_out = pltpu.make_async_copy(back_ref, out_hbm.at[:, pl.ds(0, WIDE)], out_sems.at[0])
    back_out.start()
    for c in copies[2:]:
        c.wait()
    pick = slot_matrix(idt_ref[0:1, :], slots_ref[...]).astype(bf16)[:SLOTS]
    scales = lax.dot_general(
        pick, bst_ref[...], (((1,), (1,)), ((), ())), preferred_element_type=f32
    ).astype(bf16)
    block = lax.broadcasted_iota(jnp.int32, (BLOCKS, D), 0)
    lane = lax.broadcasted_iota(jnp.int32, (BLOCKS, D), 1)
    spread = jnp.where((lane >> 7) == block, 1.0, 0.0).astype(bf16)
    deq = (dot(pick, tv_ref[...]) * dot(scales, spread)).astype(bf16)
    deq_ref[...] = deq
    deq_out = pltpu.make_async_copy(deq_ref, deq_hbm, out_sems.at[2])
    deq_out.start()
    rows_ref[...] = dot(pack, stacked(deq)).astype(bf16)
    rows_out = pltpu.make_async_copy(rows_ref, out_hbm.at[:, pl.ds(WIDE, WIDE)], out_sems.at[1])
    rows_out.start()
    deq_out.wait()
    back_out.wait()
    rows_out.wait()


def grads(idt_ref, slots_ref, og_ref, pack_ref, og_out):
    pick = slot_matrix(idt_ref[0:1, :], slots_ref[...]).astype(bf16)
    og = dot(pick[:SLOTS], og_ref[...]).astype(bf16)
    og_out[...] = dot(pack_ref[...], stacked(og)).astype(bf16)


def prepare(place_ref, idt_ref, slots_ref, ids_ref, logits_ref, deq_ref, own_out, other_out):
    pick = slot_matrix(idt_ref[0:1, :], slots_ref[...]).astype(bf16)
    logits = logits_ref[...]
    ids = ids_ref[...]
    wide_lane = lax.broadcasted_iota(jnp.int32, (TOK, EXPERTS), 1)
    lane = lax.broadcasted_iota(jnp.int32, (TOK, TOK), 1)
    chosen = jnp.zeros((TOK, TOK), f32)
    idf = jnp.zeros((TOK, TOK), f32)
    for k in range(TOPK):
        idk = ids[:, k : k + 1]
        one = jnp.sum(jnp.where(wide_lane == idk, logits, 0.0), axis=1, keepdims=True)
        chosen = jnp.where(lane == k, one, chosen)
        idf = jnp.where(lane == k, idk.astype(f32), idf)
    a = 1.0 / (1.0 + jnp.exp(-chosen))
    total = jnp.sum(jnp.where(lane < TOPK, a, 0.0), axis=1, keepdims=True)
    lead = jnp.where(lane == 0, 1.0, 0.0)
    coef = SCALE * (lead - a[:, 0:1] / total) / total * a * (1.0 - a)
    coef = jnp.where(lane < TOPK, coef, 0.0)
    high = coef.astype(bf16).astype(f32)
    low = coef - high
    meta = idf + pltpu.roll(high, TOPK, 1) + pltpu.roll(low, 2 * TOPK, 1)
    meta = jnp.transpose(dot(pick, meta.astype(bf16)))
    top = jnp.concatenate([meta[0:8], meta[8:16]], axis=1)
    bottom = jnp.concatenate([meta[16:24], jnp.zeros((8, TOK), f32)], axis=1)
    block = jnp.concatenate([top, bottom], axis=0).astype(bf16)
    deq = deq_ref[...]
    gap = jnp.zeros((SLOTS, 64 - FEAT), bf16)
    x, core = place_ref[2], place_ref[3]
    for far_x in range(RING):
        step = (far_x ^ x) & (RING - 1)
        pieces = []
        for k in (2 * far_x, 2 * far_x + 1):
            parts = []
            for q in range(CHUNKS):
                at = q * WIDE + k * FEAT
                parts += [deq[:, at : at + FEAT], gap]
            pieces.append(jnp.concatenate(parts, axis=1))
        own_out[step, :SLOTS, :] = jnp.where(core == 0, pieces[0], pieces[1])
        other_out[step, :SLOTS, :] = jnp.where(core == 0, pieces[1], pieces[0])
        own_out[step, SLOTS:, :] = block
        other_out[step, SLOTS:, :] = block


def join(own_ref, other_ref, *outs):
    for step in range(RING):
        outs[step][:ROWS, :] = own_ref[step]
        outs[step][ROWS:, :] = other_ref[step]


def gate(og_ref, got_ref, pack_ref, idt_ref, slots_ref, gate_ref, send_ref):
    prod = og_ref[...].astype(f32) * got_ref[:, :WIDE].astype(f32)
    part = prod[:, :TOK]
    for b in range(1, WIDE // TOK):
        part = part + prod[:, b * TOK : (b + 1) * TOK]
    pack = pack_ref[...].astype(f32)
    fold = pack[:, :SLOTS]
    for c in range(1, CHUNKS):
        fold = fold + pack[:, c * SLOTS : (c + 1) * SLOTS]
    fold = jnp.concatenate([fold, jnp.zeros((PACKED, TOK - SLOTS), f32)], axis=1)
    by_slot = lax.dot_general(
        part, fold, (((0,), (0,)), ((), ())), preferred_element_type=f32, precision=lax.Precision.HIGHEST
    )
    row = jnp.sum(by_slot, axis=0, keepdims=True)
    row = jnp.broadcast_to(row, (8, TOK))
    pick = slot_matrix(idt_ref[0:1, :], slots_ref[...])
    gate_ref[...] = dot(row, pick, precision=lax.Precision.HIGHEST)[0:1]
    send_ref[...] = jnp.broadcast_to(row[None, 0:1], (PEERS, 1, TOK))


def unpack(got_ref, pack_ref, out_ref):
    got = got_ref[:, WIDE:]
    for c in range(CHUNKS):
        pick = pack_ref[:, c * SLOTS : (c + 1) * SLOTS]
        out_ref[:, c * WIDE : (c + 1) * WIDE] = lax.dot_general(
            pick, got, (((0,), (0,)), ((), ())), preferred_element_type=f32
        ).astype(bf16)


def contract(place_ref, gg_ref, idt_ref, slots_ref, *refs):
    near_refs = refs[:RING]
    out_hbm, acc_ref, out_ref, out_sem = refs[RING:]
    yh, mine, x, core = (place_ref[n] for n in range(4))
    rows = lax.broadcasted_iota(jnp.int32, (EXPERTS, TOK), 0).astype(f32).astype(bf16)
    for n, step in enumerate(STEPS):
        left = []
        for o in range(2):
            at = o * ROWS + SLOTS
            meta = near_refs[n][at : at + META, :].astype(f32)
            source = ((x ^ step) & (RING - 1)) * 2 + (core ^ o)
            term = jnp.zeros((EXPERTS, TOK), bf16)
            for k in range(TOPK):
                coef = meta[k : k + 1, TOK:] + meta[8 + k : 9 + k, :TOK]
                value = (coef * gg_ref[source, 0:1, :]).astype(bf16)
                term = jnp.where(rows == meta[k : k + 1, :TOK].astype(bf16), value, term)
            left.append(term[:, :ROWS])
        part = dot(jnp.concatenate(left, axis=1), near_refs[n][...])
        if n == 0:
            acc_ref[...] = part
        else:
            acc_ref[...] += part
    lane = lax.broadcasted_iota(jnp.int32, (8, TOK), 1)
    row = lax.broadcasted_iota(jnp.int32, (8, TOK), 0)
    lead = idt_ref[0:1, :]
    pos = jnp.where(slots_ref[...] < CAP, (lead >> 4) * 8 + slots_ref[...], 1000)
    srow = lax.broadcasted_iota(jnp.int32, (TOK, TOK), 0)
    place = jnp.where(srow == pos, 1.0, 0.0)
    named = jnp.sum(place * jnp.broadcast_to(((lead & 15) + 1).astype(f32), (TOK, TOK)), axis=1, keepdims=True)
    own_lane = jnp.where(mine < 8, FEAT + mine, 64 + FEAT + mine - 8)
    left_half = lane < 64
    for j in range(PEERS):
        tag = jnp.where(lane == own_lane, named[8 * j : 8 * j + 8], 0.0)
        for h in range(2):
            lo = acc_ref[16 * j : 16 * j + 8, TOK * h : TOK * (h + 1)]
            hi = acc_ref[16 * j + 8 : 16 * j + 16, TOK * h : TOK * (h + 1)]
            first = jnp.where(left_half, lo, pltpu.roll(hi, 64, 1))
            second = jnp.where(left_half, pltpu.roll(lo, 64, 1), hi)
            out_ref[(2 * h) * PEERS + j] = (first + jnp.where(yh == 2 * h, tag, 0.0)).astype(bf16)
            out_ref[(2 * h + 1) * PEERS + j] = (second + jnp.where(yh == 2 * h + 1, tag, 0.0)).astype(bf16)

    out_copy = pltpu.make_async_copy(out_ref, out_hbm, out_sem)
    out_copy.start()
    out_copy.wait()

def finish(far_ref, grad_ref, expert_ref):
    total = jnp.sum(far_ref[...].astype(f32), axis=0)
    grad_ref[0:8, :] = total[:, :FEAT]
    grad_ref[8:16, :] = total[:, 64 : 64 + FEAT]
    lane = lax.broadcasted_iota(jnp.int32, (TOK, TOK), 0)
    slot = lax.broadcasted_iota(jnp.int32, (TOK, TOK), 1)
    source = jnp.where(lane < 64, lane - FEAT, lane - 64 - FEAT + 8)
    tagged = ((lane >= FEAT) & (lane < 64)) | (lane >= 64 + FEAT)
    first = source * CAP
    hit = tagged & (slot >= first) & (slot < first + CAP)
    spread = dot(jnp.where(lax.broadcasted_iota(jnp.int32, (8, TOK), 1) % 64 >= FEAT, total, 0.0), jnp.where(hit, 1.0, 0.0), precision=lax.Precision.HIGHEST)
    row = lax.broadcasted_iota(jnp.int32, (8, TOK), 0)
    col = lax.broadcasted_iota(jnp.int32, (8, TOK), 1)
    value = jnp.sum(jnp.where(col % CAP == row, spread, 0.0), axis=0, keepdims=True)
    expert_ref[...] = (value[:, :SLOTS] + 0.5).astype(jnp.int32) - 1


def call(body, outs, args, scratch=(), scalars=0, hbm_in=False, hbm_last=0, hbm_out=(), limit=32):
    vmem, hbm = pl.BlockSpec(memory_space=pltpu.VMEM), pl.BlockSpec(memory_space=pl.ANY)
    specs = [pl.BlockSpec(memory_space=pltpu.SMEM)] * scalars
    specs += [hbm if hbm_in else vmem] * (len(args) - scalars)
    specs[len(specs) - hbm_last :] = [hbm] * hbm_last
    return pl.pallas_call(
        body,
        out_shape=[jax.ShapeDtypeStruct(s, t) for s, t in outs],
        in_specs=specs,
        out_specs=[hbm if n in hbm_out else vmem for n in range(len(outs))],
        scratch_shapes=list(scratch),
        compiler_params=pltpu.CompilerParams(vmem_limit_bytes=limit * 2**20),
        name=body.__name__,
    )(*args)


def swap(v, axes):
    return lax.all_to_all(v, axes, split_axis=0, concat_axis=0, tiled=True)


def shards(token_values, block_scales, route_ids, route_slots, router_logits, expert_outputs, output_grad):
    pack = jnp.asarray(pack_matrix(), bf16)
    idt = route_ids.T
    slots = route_slots.reshape(1, TOK)
    place = jnp.stack(
        [lax.axis_index("yh"), lax.axis_index(OWNERS), lax.axis_index("x"), lax.axis_index("core")]
    ).astype(jnp.int32)
    out, deq = call(
        outgoing,
        [((PACKED, 2 * WIDE), bf16), ((SLOTS, D), bf16)],
        (idt, slots, token_values, block_scales.T, expert_outputs, pack),
        scratch=[
            pltpu.VMEM((TOPK, TOK), jnp.int32),
            pltpu.VMEM((1, TOK), jnp.int32),
            pltpu.VMEM((TOK, D), bf16),
            pltpu.VMEM((BLOCKS, TOK), bf16),
            pltpu.VMEM((SLOTS, D), bf16),
            pltpu.VMEM((PACKED, PACKED), bf16),
            pltpu.VMEM((PACKED, WIDE), bf16),
            pltpu.VMEM((PACKED, WIDE), bf16),
            pltpu.VMEM((SLOTS, D), bf16),
            pltpu.SemaphoreType.DMA((6,)),
            pltpu.SemaphoreType.DMA((3,)),
        ],
        hbm_in=True,
        hbm_out=(0, 1),
        limit=58,
    )
    got = swap(out, OWNERS)
    own, other = call(
        prepare,
        [((RING, ROWS, 256), bf16), ((RING, ROWS, 256), bf16)],
        (place, idt, slots, route_ids, router_logits, deq),
        scalars=1,
    )
    own, other, output_grad = lax.optimization_barrier((own, other, output_grad))
    (og,) = call(grads, [((PACKED, WIDE), bf16)], (idt, slots, output_grad, pack))
    other = lax.ppermute(other, "core", [(0, 1), (1, 0)])
    other, og = lax.optimization_barrier((other, og))
    joined = call(join, [((2 * ROWS, 256), bf16)] * RING, (own, other))
    near = [joined[0]]
    for step in STEPS[1:]:
        near.append(lax.ppermute(joined[step], "x", [(i, i ^ step) for i in range(RING)]))
    got, og, *near[:HELD] = lax.optimization_barrier((got, og, *near[:HELD]))
    gates, send = call(
        gate, [((1, TOK), f32), ((PEERS, 1, TOK), f32)], (og, got, pack, idt, slots)
    )
    gg = swap(send, NEAR)
    (expert_inputs,) = call(unpack, [((SLOTS, D), bf16)], (got, pack))
    (far,) = call(
        contract,
        [((CHUNKS * PEERS, 8, TOK), bf16)],
        (place, gg, idt, slots, *near),
        scratch=[
            pltpu.VMEM((EXPERTS, 256), f32),
            pltpu.VMEM((CHUNKS * PEERS, 8, TOK), bf16),
            pltpu.SemaphoreType.DMA,
        ],
        scalars=1,
        hbm_out=(0,),
        limit=32,
    )
    far = swap(far, FAR)
    grad, named = call(finish, [((EXP_DEV, FEAT), f32), ((1, SLOTS), jnp.int32)], (far,))
    return expert_inputs, named.reshape(SLOTS), gates.reshape(TOK), grad.T


def solution(mesh):
    fine = Mesh(mesh.devices.reshape(4, 8, 2, 8, 2), ALL)
    rows = P(ALL, None)
    return jax.shard_map(
        shards,
        mesh=fine,
        in_specs=(rows, rows, rows, P(ALL), rows, rows, rows),
        out_specs=(rows, P(ALL), P(ALL), P(("yh", "x", "core"), ("z", "yl"))),
        check_vma=False,
    )
```
